32 devices in a mesh: ctx: 8 (over y, x, core), exp: 4 (over z).
Axes of the slice: x: 2, y: 2, z: 4, core: 2. Of those that a mesh axis runs over, the one named last changes fastest.
Arguments:
- queries: bfloat16 [4096, 8192], P('ctx', 'exp'), may hold values from -6 to 6
- keys: bfloat16 [4096, 8192], P('ctx', 'exp'), may hold values from -6 to 6
- values: bfloat16 [4096, 8192], P('ctx', 'exp'), may hold values from -6 to 6
- log_decay: float32 [4096, 64], P('ctx', 'exp'), may hold values from -2 to 0, as said below
- residual: bfloat16 [4096, 3072], P(('ctx', 'exp')), may hold values from -6 to 6
- out_proj: bfloat16 [8192, 3072], P('exp'), may hold values from -0.0625 to 0.0625
- expert_ids: int32 [4096, 2], P(('ctx', 'exp')), may hold values from 0 to 15, all different within a row; in each aligned block of 128 rows (0 to 127, 128 to 255, ...) at most 20 rows name the same one
- route_weights: float32 [4096, 2], P(('ctx', 'exp')), may hold values from 0.1 to 0.9
- w_gate: bfloat16 [16, 3072, 6144], P('exp', None, 'ctx'), may hold values from -0.109375 to 0.109375
- w_up: bfloat16 [16, 3072, 6144], P('exp', None, 'ctx'), may hold values from -0.109375 to 0.109375
- w_down: bfloat16 [16, 6144, 3072], P('exp', 'ctx'), may hold values from -0.078125 to 0.078125
Outputs:
- mixed: bfloat16 [4096, 3072], P(('ctx', 'exp'))
The draws below stay inside these ranges and needn't reach their ends.
Inputs may be any that keep to these rules, and one draw needn't show every extreme that they name: `expert_ids`: each token names two different experts. In each aligned block of 128 tokens no expert is named more than 20 times, and in some blocks one expert is named exactly 20 times. `log_decay`: every entry is negative.
All inputs are finite; a program needn't handle non-finite values.
Results may differ from the reference program's by a relative error of at most 0.019.
Values may be sent and summed in bfloat16 or wider, within the bound.
A program may use at most 192 MiB of HBM per device.

```python
import math
import jax
import jax.numpy as jnp
import numpy as np
from jax import lax

D = 3072
HEADS = 64
HD = 128
EXPERTS = 16
FF = 6144
TOK_DEV = 512
TOKENS = 4096
MTOK = 128
CAP = 20
N_CTX = 8
N_EXP = 4


def draw_log_decay(key, part):
    keys_all = jax.random.split(jax.random.fold_in(key, 7717), 7)
    picks = jax.random.randint(keys_all[0], (HEADS,), 0, 16)
    fast = picks < 8
    fast_rate = jnp.exp(jax.random.uniform(keys_all[1], (HEADS,), jnp.float32, math.log(1.0 / 50.0), math.log(1.0 / 30.0)))
    slow_rate = jnp.exp(jax.random.uniform(keys_all[2], (HEADS,), jnp.float32, math.log(0.05), math.log(0.3))) / TOKENS
    base = jnp.where(fast, fast_rate, slow_rate)
    block_count = TOKENS // TOK_DEV
    block_factor = jnp.exp(jax.random.uniform(keys_all[3], (block_count, HEADS), jnp.float32, math.log(0.6), math.log(1.5)))
    token_factor = jnp.exp(jax.random.uniform(keys_all[4], (TOKENS, HEADS), jnp.float32, math.log(0.5), math.log(1.5)))
    forgetting_factor = base[None, :] * jnp.repeat(block_factor, TOK_DEV, axis=0) * token_factor
    spots = jax.random.randint(keys_all[5], (2, HEADS), 0, TOKENS)
    layer_number = jax.random.uniform(keys_all[6], (2, HEADS), jnp.float32, 0.2, 0.5)
    place = jnp.arange(TOKENS, dtype=jnp.int32)
    assignment_tally = place[:, None, None] == spots[None, :, :]
    sequence_pieces = jnp.sum(jnp.where(assignment_tally, jnp.log(1.0 - layer_number)[None, :, :], 0.0), axis=1)
    return (sequence_pieces - forgetting_factor).astype(jnp.float32)


def steps_of(rng, dims, pieces, low, high):
    level, own = 1.0, jax.random.fold_in(rng, 6)
    for position, shards_of in pieces:
        draws = jnp.exp(jax.random.uniform(jax.random.fold_in(own, position), (shards_of,), jnp.float32, low / len(pieces), high / len(pieces)))
        level = level * jnp.repeat(draws, dims[position] // shards_of).reshape([-1 if axis == position else 1 for axis in range(len(dims))])
    return level


def assign_block(own_key, own, number, rows, amount, top, bound, slope):
    order = jax.random.permutation(own_key, amount)
    crowded, ordinary = portions_of(amount, rows * top, bound, slope, True), portions_of(amount, rows * top, bound, slope, False)
    places = jnp.arange(amount)

    def named(lengths, turn):
        used = int((lengths > 0).sum())
        fixed = max(1, used // 4)
        shifted = fixed + (places - fixed + turn * (used - fixed)) % max(1, amount - fixed)
        return jnp.zeros((amount,), jnp.int32).at[order[jnp.where(places < fixed, places, shifted)]].set(jnp.asarray(lengths, jnp.int32))

    lengths = jnp.where(number % 4 == 0, named(crowded, number // 4), named(ordinary, number - number // 4 - 1))
    mixed = jax.random.permutation(jax.random.fold_in(own, 3), amount)
    donor, sink = mixed[0:amount // 2 * 2:2], mixed[1:amount // 2 * 2:2]
    room = jnp.minimum(lengths[donor] - 1, bound - lengths[sink]) // 2
    room = jnp.where((donor == order[0]) | (sink == order[0]) | (lengths[sink] == 0), 0, jnp.maximum(room, 0))
    shifted = jax.random.randint(jax.random.fold_in(own, 4), (amount // 2,), 0, 1 << 20) % (room + 1)
    lengths = lengths.at[donor].add(-shifted).at[sink].add(shifted)
    members = jnp.searchsorted(jnp.cumsum(lengths), jnp.arange(rows * top), side="right").astype(jnp.int32)
    grid = members.reshape(top, rows).T
    grid = grid[jax.random.permutation(jax.random.fold_in(own, 1), rows)]
    turn = jax.random.randint(jax.random.fold_in(own, 2), (rows, 1), 0, top)
    return jnp.take_along_axis(grid, (jnp.arange(top)[None, :] + turn) % top, axis=1)


def portions_of(amount, total, most, lean, full):
    portions = [(1 << 20) // math.isqrt(rank ** lean) + 1 for rank in range(1, amount + 1)]
    largest = most if full else min(most, max(-(-total // amount), total * portions[0] // sum(portions)))
    least = 1 if total - largest >= amount - 1 else 0
    holding, spare = [largest] + [least] * (amount - 1), total - largest - least * (amount - 1)
    while spare > 0:
        free = [i for i in range(1, amount) if holding[i] < largest] or [i for i in range(1, amount) if holding[i] < most]
        mass, left = sum([portions[i] for i in free]), spare
        for i in free:
            more = min(most - holding[i], max(1, left * portions[i] // mass), spare)
            holding[i] = holding[i] + more
            spare = spare - more
    return np.array(holding)


def gaussian(stream_key, dims, width, most, pieces=(), held_as=jnp.bfloat16):
    drawn = width * jax.random.normal(stream_key, dims, jnp.float32)
    if pieces:
        drawn = drawn * steps_of(stream_key, dims, pieces, -0.22, 0.18)
    return jnp.clip(drawn, -most, most).astype(held_as)


def setup_inputs(seed: int = 0) -> dict:
    streams_of = jax.random.split(jax.random.key(seed), 12)
    queries = gaussian(streams_of[0], (TOKENS, HEADS * HD), 1.0, 6.0, ((0, 8), (1, 4)))
    keys = gaussian(streams_of[1], (TOKENS, HEADS * HD), 1.0, 6.0, ((0, 8), (1, 4)))
    values = gaussian(streams_of[2], (TOKENS, HEADS * HD), 1.0, 6.0, ((0, 8), (1, 4)))
    log_decay = draw_log_decay(jax.random.fold_in(streams_of[11], 71), 0)
    residual = gaussian(streams_of[4], (TOKENS, D), 1.0, 6.0, ((0, 32),))
    out_proj = gaussian(streams_of[5], (HEADS * HD, D), (HEADS * HD) ** -0.5, 0.0625, ((0, 4),))
    expert_ids_keys = jax.random.split(jax.random.fold_in(streams_of[6], 1), TOKENS // MTOK)
    expert_ids_turns = jax.random.permutation(jax.random.fold_in(streams_of[6], 3), TOKENS // MTOK)
    expert_ids = jax.vmap(lambda own, number: assign_block(jax.random.fold_in(streams_of[6], 2), own, number, MTOK, EXPERTS, 2, CAP, 2))(expert_ids_keys, expert_ids_turns).reshape((TOKENS, 2))
    route_weights = jnp.clip(0.1 + 0.79999997 * jax.random.uniform(streams_of[7], (TOKENS, 2), jnp.float32) ** steps_of(streams_of[7], (TOKENS, 2), ((0, 32),), -0.2, 0.2), 0.1, 0.9)
    w_gate = gaussian(streams_of[8], (EXPERTS, D, FF), D ** -0.5, 0.109375, ((0, 4), (2, 8)))
    w_up = gaussian(streams_of[9], (EXPERTS, D, FF), D ** -0.5, 0.109375, ((0, 4), (2, 8)))
    w_down = gaussian(streams_of[10], (EXPERTS, FF, D), FF ** -0.5, 0.078125, ((0, 4), (1, 8)))
    return dict(queries=queries, keys=keys, values=values, log_decay=log_decay, residual=residual, out_proj=out_proj, expert_ids=expert_ids, route_weights=route_weights, w_gate=w_gate, w_up=w_up, w_down=w_down)


EPS = 1e-06

def attend_block(carried, block):
    qb, kb, vb, ab = block
    cum = jnp.cumsum(ab, axis=0)
    qf = qb.astype(jnp.float32)
    kf = kb.astype(jnp.float32)
    vf = vb.astype(jnp.float32)
    scores = jnp.einsum('thd,shd->hts', qf, kf, precision=lax.Precision.HIGHEST)
    place = jnp.arange(qb.shape[0], dtype=jnp.int32)
    causal = (place[:, None] >= place[None, :])[None]
    diff = cum.T[:, :, None] - cum.T[:, None, :]
    weights = jnp.where(causal, scores * jnp.exp(jnp.where(causal, diff, 0.0)), 0.0).astype(jnp.bfloat16)
    intra = jnp.einsum('hts,shd->thd', weights.astype(jnp.float32), vf, precision=lax.Precision.HIGHEST)
    inter = jnp.exp(cum)[:, :, None] * jnp.einsum('thd,hde->the', qf, carried, precision=lax.Precision.HIGHEST)
    attn = intra + inter
    last = cum[-1]
    scaled_keys = (kf * jnp.exp(last[None, :] - cum)[:, :, None]).astype(jnp.bfloat16)
    state = jnp.einsum('thd,the->hde', scaled_keys.astype(jnp.float32), vf, precision=lax.Precision.HIGHEST)
    new_carried = jnp.exp(last)[:, None, None] * carried + state
    normed = (attn * lax.rsqrt(lax.optimization_barrier(jnp.mean(attn * attn, axis=-1, keepdims=True)) + EPS)).astype(jnp.bfloat16)
    return (new_carried, normed)

def reference(queries, keys, values, log_decay, residual, out_proj, expert_ids, route_weights, w_gate, w_up, w_down):
    shaped = (N_CTX, TOK_DEV, HEADS, HD)
    blocks = (queries.reshape(shaped), keys.reshape(shaped), values.reshape(shaped), log_decay.reshape(N_CTX, TOK_DEV, HEADS))
    start_state = jnp.zeros((HEADS, HD, HD), jnp.float32)
    _, normed = lax.scan(attend_block, start_state, blocks)
    normed = normed.reshape(TOKENS, HEADS * HD)
    group = HEADS * HD // N_EXP

    def add_group(total, index):
        begin = (index * group).astype(jnp.int32)
        part = jnp.dot(lax.dynamic_slice_in_dim(normed, begin, group, 1), lax.dynamic_slice_in_dim(out_proj, begin, group, 0), preferred_element_type=jnp.float32).astype(jnp.bfloat16)
        part = lax.optimization_barrier(part)
        return (total + part.astype(jnp.float32), None)
    proj, _ = lax.scan(add_group, jnp.zeros((TOKENS, D), jnp.float32), jnp.arange(N_EXP, dtype=jnp.int32))
    feature_vector = residual.astype(jnp.float32) + proj
    moe_in = (feature_vector * lax.rsqrt(lax.optimization_barrier(jnp.mean(feature_vector * feature_vector, axis=-1, keepdims=True)) + EPS)).astype(jnp.bfloat16)
    flat_ids = expert_ids.reshape(-1)
    most_rows = N_CTX * N_EXP * CAP
    slice_units = FF // N_CTX

    def per_expert(expert):
        order = jnp.argsort(jnp.where(flat_ids == expert, 0, 1).astype(jnp.int32), stable=True)[:most_rows].astype(jnp.int32)
        valid = jnp.take(flat_ids, order) == expert
        rows = jnp.take(moe_in, order // 2, axis=0)
        gate = jnp.dot(rows, w_gate[expert], preferred_element_type=jnp.float32)
        upper = jnp.dot(rows, w_up[expert], preferred_element_type=jnp.float32)
        act = (jax.nn.silu(gate) * upper).astype(jnp.bfloat16)
        parts = jnp.einsum('mcf,cfd->mcd', act.reshape(most_rows, N_CTX, slice_units).astype(jnp.float32), w_down[expert].reshape(N_CTX, slice_units, D).astype(jnp.float32), precision=lax.Precision.HIGHEST)
        parts = lax.optimization_barrier(parts.astype(jnp.bfloat16))
        out = lax.optimization_barrier(jnp.sum(parts.astype(jnp.float32), axis=1)).astype(jnp.bfloat16)
        target = jnp.where(valid, order, 2 * TOKENS).astype(jnp.int32)
        return (target, out)
    target_experts, outs = lax.map(per_expert, jnp.arange(EXPERTS, dtype=jnp.int32))
    expert_out = jnp.zeros((2 * TOKENS, D), jnp.bfloat16).at[target_experts.reshape(-1)].set(outs.reshape(-1, D), mode='drop')
    expert_out = expert_out.astype(jnp.float32).reshape(TOKENS, 2, D)
    moe = route_weights[:, 0:1] * expert_out[:, 0] + route_weights[:, 1:2] * expert_out[:, 1]
    return (feature_vector + moe).astype(jnp.bfloat16)
```

```python
import jax
import jax.numpy as jnp
from jax import lax
from jax.experimental import pallas as pl
from jax.experimental.pallas import tpu as pltpu
from jax.sharding import PartitionSpec as P

EPS = 1e-06


def prefix(shard, axis, combine, identity):
    length, here = (lax.axis_size(axis), lax.axis_index(axis))
    everything = jax.tree.map(
        lambda part, kind: lax.all_gather(part.astype(kind), axis),
        shard,
        (jnp.bfloat16, jnp.bfloat16),
    )
    start = jax.tree.map(
        lambda part, zero: jnp.broadcast_to(jnp.asarray(zero, part.dtype), part.shape),
        shard,
        identity,
    )

    def hop(k, before):
        reached = k < here
        new = combine(
            before, jax.tree.map(lambda part, own: part[k].astype(own.dtype), everything, shard)
        )
        return jax.tree.map(lambda a, b: jnp.where(reached, a, b), new, before)

    return lax.fori_loop(0, length, hop, start)


def chain_combine(earlier, later):
    return (earlier[0] + later[0], jnp.exp(later[0])[:, None, None] * earlier[1] + later[1])


def slot_table(chosen_specialist_index, capacity, local_experts, experts, tiled):
    flat = chosen_specialist_index.reshape(-1)
    onehot = (flat[:, None] == jnp.arange(experts, dtype=jnp.int32)[None, :]).astype(jnp.int32)
    earlier = jnp.tri(flat.shape[0], k=-1, dtype=jnp.bfloat16)
    preceding_sum = jnp.dot(
        earlier, onehot.astype(jnp.bfloat16), preferred_element_type=jnp.float32
    ).astype(jnp.int32)
    position = jnp.sum(preceding_sum * onehot, axis=1)
    if tiled:
        few = capacity - TILE
        here = flat % local_experts
        slots = flat // local_experts * (capacity * local_experts) + jnp.where(
            position < TILE,
            few * local_experts + TILE * here + position,
            few * here + position - TILE,
        )
        return slots.reshape(chosen_specialist_index.shape)
    slots = (
        flat // local_experts * (capacity * local_experts)
        + position * local_experts
        + flat % local_experts
    )
    return slots.reshape(chosen_specialist_index.shape)


def dispatch_table(slots, total_slots):
    assignment_tally = slots[None, :, :] == jnp.arange(total_slots, dtype=jnp.int32)[:, None, None]
    return jnp.any(assignment_tally, axis=2).astype(jnp.bfloat16)


TILE = 16
PARTS = 5


def expert_kernel(
    packed, w_gate, w_up, w_down, out,
    rows, extra, acts, extra_acts, pair, diag_x, diag_y, sum_x, sum_y, final, w_in, w_out,
    z_send, z_recv, g_send, g_recv, r_send, r_recv, b_send, b_recv, w_sem, d_sem,
):
    me, z = lax.axis_index("ctx"), lax.axis_index("exp")
    core, x, y = me % 2, (me // 2) % 2, me // 4
    mate = (me + 1 - 2 * core, z)
    x_near = (me + 2 - 4 * x, z)
    y_near = (me + 4 - 8 * y, z)
    others = [(me, (z + k) % 4) for k in (1, 2, 3)]
    block, width = rows.shape[3], rows.shape[4]
    half = block // 2
    experts = w_gate.shape[0]
    hidden = w_gate.shape[2]
    tile, wide = w_in.shape[3], w_out.shape[2]
    tiles, wides = hidden // tile, width // wide
    top, bottom = pl.ds(0, half), pl.ds(half, half)

    barrier = pltpu.get_barrier_semaphore()
    for device in [mate, x_near, y_near] + others:
        pl.semaphore_signal(
            barrier, inc=1, device_id=device, device_id_type=pl.DeviceIdType.MESH
        )
    pl.semaphore_wait(barrier, 6)

    def remote(src, dst, send, recv, device):
        return pltpu.make_async_remote_copy(
            src_ref=src, dst_ref=dst, send_sem=send, recv_sem=recv,
            device_id=device, device_id_type=pl.DeviceIdType.MESH,
        )

    def part_rows(p):
        return pl.ds(pl.multiple_of(p * TILE, TILE), TILE)

    def z_copy(p, k):
        return remote(
            packed.at[others[k][1], part_rows(p)], rows.at[p, 0, 0, part_rows(z)],
            z_send.at[p, k], z_recv.at[p, k], others[k],
        )

    def g_copy(p, k):
        src, dst, device = (
            lambda: (rows.at[p, 0, 0], rows.at[p, 0, 1], x_near),
            lambda: (rows.at[p, 0, 0], rows.at[p, 0, 2], y_near),
            lambda: (rows.at[p, 0, 0], rows.at[p, 1, 0], mate),
            lambda: (rows.at[p, 0, 1, top], rows.at[p, 0, 3, top], y_near),
            lambda: (rows.at[p, 0, 2, bottom], rows.at[p, 0, 3, bottom], x_near),
            lambda: (rows.at[p, 0, 1], rows.at[p, 1, 1], mate),
            lambda: (rows.at[p, 0, 2], rows.at[p, 1, 2], mate),
            lambda: (rows.at[p, 0, 3], rows.at[p, 1, 3], mate),
        )[k]()
        return remote(src, dst, g_send.at[p, k], g_recv.at[p, k], device)

    def r_copy(p, k):
        src, dst, device = (
            lambda: (rows.at[p, 1], pair.at[p], mate),
            lambda: (rows.at[p, 0, 3, top], diag_x.at[p], x_near),
            lambda: (rows.at[p, 0, 3, bottom], diag_y.at[p], y_near),
            lambda: (rows.at[p, 0, 1], sum_x.at[p], x_near),
            lambda: (rows.at[p, 0, 2], sum_y.at[p], y_near),
        )[k]()
        return remote(src, dst, r_send.at[p, k], r_recv.at[p, k], device)

    def b_copy(p, k):
        return remote(
            final.at[p, part_rows(others[k][1])], out.at[z, part_rows(p)],
            b_send.at[p, k], b_recv.at[p, k], others[k],
        )

    def gather_1(p):
        for k in range(3):
            z_copy(p, k).wait_recv()
        for k in (0, 1, 2):
            g_copy(p, k).start()

    def gather_2(p):
        g_copy(p, 0).wait_recv()
        g_copy(p, 3).start()
        g_copy(p, 5).start()
        g_copy(p, 1).wait_recv()
        g_copy(p, 4).start()
        g_copy(p, 6).start()

    def gather_3(p):
        g_copy(p, 3).wait_recv()
        g_copy(p, 4).wait_recv()
        g_copy(p, 7).start()

    def gather_4(p):
        for k in (2, 5, 6, 7):
            g_copy(p, k).wait_recv()

    def gather_sent(p):
        for k in range(8):
            g_copy(p, k).wait_send()

    def add(a, b):
        return a.astype(jnp.float32) + b.astype(jnp.float32)

    def reduce_1(p):
        r_copy(p, 0).start()

    def reduce_2(p):
        r_copy(p, 0).wait_recv()
        for q in (3, 1, 2, 0):
            rows[p, 0, q] = add(rows[p, 0, q], pair[p, q]).astype(jnp.bfloat16)
            if q == 3:
                r_copy(p, 1).start()
                r_copy(p, 2).start()

    def reduce_3(p):
        r_copy(p, 1).wait_recv()
        rows[p, 0, 2, top] = add(rows[p, 0, 2, top], diag_x[p]).astype(jnp.bfloat16)
        r_copy(p, 4).start()
        r_copy(p, 2).wait_recv()
        rows[p, 0, 1, bottom] = add(rows[p, 0, 1, bottom], diag_y[p]).astype(jnp.bfloat16)
        r_copy(p, 3).start()

    def reduce_4(p):
        r_copy(p, 3).wait_recv()
        r_copy(p, 4).wait_recv()
        total = add(rows[p, 0, 0], sum_x[p]) + sum_y[p].astype(jnp.float32)
        final[p] = total.astype(jnp.bfloat16)
        for k in range(3):
            b_copy(p, k).start()
        out[z, part_rows(p)] = final[p, part_rows(z)]

    def in_copies(n):
        e, cols = n // tiles, pl.ds(pl.multiple_of((n % tiles) * tile, tile), tile)
        return [
            pltpu.make_async_copy(w.at[e, :, cols], w_in.at[n % 2, i], w_sem.at[n % 2, i])
            for i, w in enumerate((w_gate, w_up))
        ]

    def out_copy(n):
        cols = pl.ds(pl.multiple_of((n % wides) * wide, wide), wide)
        return pltpu.make_async_copy(
            w_down.at[n // wides, :, cols], w_out.at[n % 2], d_sem.at[n % 2]
        )

    for p in range(PARTS):
        for k in range(3):
            z_copy(p, k).start()
    for n in range(2):
        for copy in in_copies(n):
            copy.start()
        out_copy(n).start()
    for p in range(PARTS):
        rows[p, 0, 0, part_rows(z)] = packed[z, part_rows(p)]

    gather_1(0)
    gather_1(1)
    gather_2(0)
    gather_1(2)
    gather_2(1)
    gather_3(0)
    gather_4(0)

    total_rows = 8 * block
    per = total_rows // experts
    few = TILE // experts
    here = lax.broadcasted_iota(jnp.int32, (total_rows, total_rows), 0)
    there = lax.broadcasted_iota(jnp.int32, (total_rows, total_rows), 1)

    place = ((here % per) // few) * TILE + (here // per) * few + here % few
    pick = (place == there).astype(jnp.bfloat16)

    @pl.loop(0, wides)
    def _(n):
        cols = pl.ds(pl.multiple_of(n * wide, wide), wide)
        had = rows[0, :, :, :, cols].reshape(total_rows, wide)
        extra[:, :, cols] = (
            jnp.dot(pick, had, preferred_element_type=jnp.float32)
            .astype(jnp.bfloat16)
            .reshape(experts, per, wide)
        )

    gather_3(1)
    gather_1(3)

    def silu_times(a, n):
        gate = jnp.dot(a, w_in[n % 2, 0], preferred_element_type=jnp.float32)
        upper = jnp.dot(a, w_in[n % 2, 1], preferred_element_type=jnp.float32)
        return (gate / (1.0 + jnp.exp(-gate)) * upper).astype(jnp.bfloat16)

    @pl.loop(0, experts)
    def _(e):
        p = e + 1
        gather_4(p)

        @pl.loop(0, tiles)
        def _(s):
            n = e * tiles + s
            for copy in in_copies(n):
                copy.wait()
            acts[s] = silu_times(rows[p].reshape(total_rows, width), n)
            extra_acts[s] = silu_times(extra[e], n)

            @pl.when(n + 2 < experts * tiles)
            def _():
                for copy in in_copies(n + 2):
                    copy.start()

            @pl.when((s == 0) & (e < experts - 1))
            def _():
                gather_2(p + 1)

            @pl.when((s == 0) & (e == 0))
            def _():
                gather_1(4)

            @pl.when((s == 1) & (e < experts - 1))
            def _():
                gather_3(p + 1)

            @pl.when((s == 0) & (e > 0))
            def _():
                reduce_2(p - 1)

            @pl.when((s == 1) & (e > 0))
            def _():
                reduce_3(p - 1)

            @pl.when((s == 2) & (e > 0))
            def _():
                reduce_4(p - 1)

        gather_sent(p)

        @pl.loop(0, wides)
        def _(s):
            n = e * wides + s
            out_copy(n).wait()
            cols = pl.ds(pl.multiple_of(s * wide, wide), wide)

            def down(ref):
                return sum(
                    jnp.dot(
                        ref[i], w_out[n % 2, i * tile:(i + 1) * tile, :],
                        preferred_element_type=jnp.float32,
                    )
                    for i in range(tiles)
                ).astype(jnp.bfloat16)

            rows[p, :, :, :, cols] = down(acts).reshape(2, 4, block, wide)
            extra[e, :, cols] = down(extra_acts)

            @pl.when(n + 2 < experts * wides)
            def _():
                out_copy(n + 2).start()

        reduce_1(p)

    gather_sent(0)
    back = ((there % per) // few) * TILE + (there // per) * few + there % few
    unpick = (back == here).astype(jnp.bfloat16)

    @pl.loop(0, wides)
    def _(n):
        cols = pl.ds(pl.multiple_of(n * wide, wide), wide)
        made = extra[:, :, cols].reshape(total_rows, wide)
        rows[0, :, :, :, cols] = (
            jnp.dot(unpick, made, preferred_element_type=jnp.float32)
            .astype(jnp.bfloat16)
            .reshape(2, 4, block, wide)
        )

    reduce_1(0)
    for stage in (reduce_2, reduce_3, reduce_4):
        stage(4)
        stage(0)
    for p in range(PARTS):
        for k in range(3):
            z_copy(p, k).wait_send()
            b_copy(p, k).wait()
        for k in range(5):
            r_copy(p, k).wait_send()


def expert_layer(packed, w_gate, w_up, w_down):
    experts, width, hidden = w_gate.shape
    block = 4 * TILE
    tile, wide = hidden // 3, width // 3
    bf16, dma = jnp.bfloat16, pltpu.SemaphoreType.DMA
    anywhere = pl.BlockSpec(memory_space=pl.ANY)
    vmem = pl.BlockSpec(memory_space=pltpu.VMEM)
    return pl.pallas_call(
        expert_kernel,
        out_shape=jax.ShapeDtypeStruct(packed.shape, bf16),
        in_specs=[vmem, anywhere, anywhere, anywhere],
        out_specs=vmem,
        scratch_shapes=[
            pltpu.VMEM((PARTS, 2, 4, block, width), bf16),
            pltpu.VMEM((experts, 8 * block // experts, width), bf16),
            pltpu.VMEM((3, 8 * block, tile), bf16),
            pltpu.VMEM((3, 8 * block // experts, tile), bf16),
            pltpu.VMEM((PARTS, 4, block, width), bf16),
            pltpu.VMEM((PARTS, block // 2, width), bf16),
            pltpu.VMEM((PARTS, block // 2, width), bf16),
            pltpu.VMEM((PARTS, block, width), bf16),
            pltpu.VMEM((PARTS, block, width), bf16),
            pltpu.VMEM((PARTS, block, width), bf16),
            pltpu.VMEM((2, 2, width, tile), bf16),
            pltpu.VMEM((2, hidden, wide), bf16),
            dma((PARTS, 3)), dma((PARTS, 3)),
            dma((PARTS, 8)), dma((PARTS, 8)),
            dma((PARTS, 5)), dma((PARTS, 5)),
            dma((PARTS, 3)), dma((PARTS, 3)),
            dma((2, 2)), dma((2,)),
        ],
        compiler_params=pltpu.CompilerParams(
            collective_id=0, has_side_effects=True, vmem_limit_bytes=60 * 1024 * 1024
        ),
    )(packed, w_gate, w_up, w_down)


def on_device(
    queries,
    keys,
    values,
    log_decay,
    residual,
    out_proj,
    expert_ids,
    route_weights,
    w_gate,
    w_up,
    w_down,
):
    tok = queries.shape[0]
    heads_here = log_decay.shape[1]
    head_dim = queries.shape[1] // heads_here
    q_heads = queries.reshape(tok, heads_here, head_dim)
    k_heads = keys.reshape(tok, heads_here, head_dim)
    v_heads = values.reshape(tok, heads_here, head_dim)
    cum = jnp.dot(
        jnp.tri(tok, dtype=jnp.float32), log_decay, precision=lax.Precision.HIGHEST
    )
    scores = jnp.einsum("thd,shd->hts", q_heads, k_heads, preferred_element_type=jnp.float32)
    place = jnp.arange(tok, dtype=jnp.int32)
    causal = (place[:, None] >= place[None, :])[None]
    diff = cum.T[:, :, None] - cum.T[:, None, :]
    weights = jnp.where(causal, scores * jnp.exp(jnp.where(causal, diff, 0.0)), 0.0).astype(
        jnp.bfloat16
    )
    intra = jnp.einsum("hts,shd->thd", weights, v_heads, preferred_element_type=jnp.float32)
    last = cum[-1]
    scaled_keys = (k_heads.astype(jnp.float32) * jnp.exp(last[None, :] - cum)[:, :, None]).astype(
        jnp.bfloat16
    )
    summary = jnp.einsum("thd,the->hde", scaled_keys, v_heads, preferred_element_type=jnp.float32)
    _, carried = prefix(
        (last, summary), "ctx", chain_combine, (jnp.zeros_like(last), jnp.zeros_like(summary))
    )
    inter = jnp.exp(cum)[:, :, None] * jnp.einsum(
        "thd,hde->the", q_heads.astype(jnp.float32), carried, precision=lax.Precision.HIGHEST
    )
    attn = intra + inter
    normed = (
        (attn * lax.rsqrt(jnp.mean(attn * attn, axis=-1, keepdims=True) + EPS))
        .astype(jnp.bfloat16)
        .reshape(tok, heads_here * head_dim)
    )
    n_exp = lax.axis_size("exp")
    proj = lax.psum_scatter(
        jnp.dot(normed, out_proj, preferred_element_type=jnp.float32).astype(jnp.bfloat16),
        "exp",
        scatter_dimension=0,
        tiled=True,
    ).astype(jnp.float32)
    feature_vector = residual.astype(jnp.float32) + proj
    moe_in = (
        feature_vector
        * lax.rsqrt(jnp.mean(feature_vector * feature_vector, axis=-1, keepdims=True) + EPS)
    ).astype(jnp.bfloat16)
    local_experts = w_gate.shape[0]
    experts = local_experts * n_exp
    mtok = residual.shape[0]
    width = residual.shape[1]
    capacity = max(2, (5 * mtok + 2 * experts - 1) // (2 * experts))
    total_slots = experts * capacity
    n_ctx = lax.axis_size("ctx")
    tiled = (n_ctx, n_exp, local_experts, capacity) == (8, 4, 4, TILE + 4)
    local_slot_table = slot_table(expert_ids, capacity, local_experts, experts, tiled)
    packed = jnp.dot(
        dispatch_table(local_slot_table, total_slots), moe_in, preferred_element_type=jnp.float32
    ).astype(jnp.bfloat16)
    if tiled:
        returned = expert_layer(
            packed.reshape(n_exp, capacity * local_experts, width), w_gate, w_up, w_down
        ).reshape(total_slots, width)
    else:
        packed = packed.reshape(n_exp, capacity, local_experts, width)
        arrived = lax.all_to_all(packed, "exp", split_axis=0, concat_axis=1, tiled=True).reshape(
            n_exp * capacity, local_experts, width
        )
        piece = lax.all_gather(arrived, "ctx", axis=0, tiled=True)
        gate = jnp.einsum("red,edf->ref", piece, w_gate, preferred_element_type=jnp.float32)
        upper = jnp.einsum("red,edf->ref", piece, w_up, preferred_element_type=jnp.float32)
        acts = (jax.nn.silu(gate) * upper).astype(jnp.bfloat16)
        summed = lax.psum_scatter(
            jnp.einsum("ref,efd->red", acts, w_down, preferred_element_type=jnp.float32).astype(
                jnp.bfloat16
            ),
            "ctx",
            scatter_dimension=0,
            tiled=True,
        )
        outgoing = summed.reshape(n_exp, capacity, local_experts, width)
        returned = lax.all_to_all(outgoing, "exp", split_axis=0, concat_axis=0, tiled=True).reshape(
            total_slots, width
        )
    picker = (
        local_slot_table.reshape(-1)[:, None] == jnp.arange(total_slots, dtype=jnp.int32)[None, :]
    ).astype(jnp.bfloat16)
    fetched = jnp.dot(picker, returned, preferred_element_type=jnp.float32).reshape(mtok, 2, width)
    moe = route_weights[:, 0:1] * fetched[:, 0] + route_weights[:, 1:2] * fetched[:, 1]
    return (feature_vector + moe).astype(jnp.bfloat16)


def solution(mesh):
    placed = (
        P("ctx", "exp"),
        P("ctx", "exp"),
        P("ctx", "exp"),
        P("ctx", "exp"),
        P(("ctx", "exp"), None),
        P("exp", None),
        P(("ctx", "exp"), None),
        P(("ctx", "exp"), None),
        P("exp", None, "ctx"),
        P("exp", None, "ctx"),
        P("exp", "ctx", None),
    )
    return jax.shard_map(
        on_device, mesh=mesh, in_specs=placed, out_specs=P(("ctx", "exp"), None), check_vma=False
    )
```
